32 devices in a mesh: fsdp: 16 (over z, x, core), dp: 2 (over y).
Axes of the slice: x: 2, y: 2, z: 4, core: 2. Of those that a mesh axis runs over, the one named last changes fastest.
Arguments:
- projected: bfloat16 [20480, 4992], P(('fsdp', 'dp')), may hold values from -24 to 24
- cotangent: bfloat16 [20480, 3200], P(('fsdp', 'dp')), may hold values from -6 to 6
- out_weight: float32 [1664, 3200], P('fsdp'), may hold values from -0.15625 to 0.15625
- clip_counts: int32 [64], P(('fsdp', 'dp')), may hold values from 192 to 320, as said below
- tube_index: int32 [20480], P(('fsdp', 'dp')), may hold values from 0 to 2047, as said below
Outputs:
- out_rows: bfloat16 [20480, 3200], P(('fsdp', 'dp'))
- grad_projected: bfloat16 [20480, 4992], P(('fsdp', 'dp'))
- grad_weight: float32 [1664, 3200], P('fsdp')
The draws below stay inside these ranges and needn't reach their ends.
Inputs may be any that keep to these rules, and one draw needn't show every extreme that they name: `clip_counts`: entry b * 2 + j counts the visible tubes of clip j of row block b. Row blocks 2p and 2p+1 together hold at most 1024 visible tubes, and some such pair holds exactly 1024; some clip holds 320. `tube_index`: within a clip the kept tube indices are distinct and ascending; a block's clips stand end to end from the block's first row, and rows after a block's last visible tube hold 0.
All inputs are finite; a program needn't handle non-finite values.
Results may differ from the reference program's by a relative error of at most 0.0018.
The reference program's roundings to bfloat16 on the way (of `weight_copy`, `probs_low`, `attn`, `masked_cot`, `grad_attn`, `grad_values` and `grad_scores`) count: a program that leaves them out, or rounds other values in their place, can miss the bound.
Values may be sent and summed in bfloat16 or wider, within the bound.
A program may use at most 192 MiB of HBM per device.

```python
import jax
import jax.numpy as jnp
import numpy as np
from jax import lax

D = 3200
H = 13
HS = 128
HD = 1664
TSTEPS = 8
GRID = 16
CAP = 320
CLIP_DEV = 2
ROWS_DEV = 640
PAIR_ROWS = 1024
ROWS = 20480
N_FSDP = 16
N_DP = 2


def pair_counts(key):
    pairs = N_FSDP
    lowest = CAP * 3 // 5
    spread = CAP - lowest
    first_key, slack_key, order_key, split_key = jax.random.split(key, 4)
    pair_number = jnp.arange(pairs)
    clip_number = jnp.arange(CLIP_DEV)
    first = jax.random.randint(first_key, (pairs, CLIP_DEV), lowest, CAP + 1, dtype=jnp.int32)
    first = jnp.where(pair_number[:, None] == 0, CAP, first)
    first = jnp.where((pair_number[:, None] == 1) & (clip_number[None, :] == 0), lowest, first)
    first_total = jnp.sum(first, axis=1)
    slack = jax.random.randint(slack_key, (pairs,), 0, CAP // 10 + 1, dtype=jnp.int32)
    slack = jnp.minimum(slack, CLIP_DEV * CAP - first_total)
    slack = jnp.where(pair_number == 0, 0, slack)
    extra = PAIR_ROWS - first_total - slack - lowest * CLIP_DEV
    split_keys = jax.random.split(split_key, CLIP_DEV)
    shares = []
    for clip in range(CLIP_DEV - 1):
        later = CLIP_DEV - 1 - clip
        floor_part = jnp.maximum(0, extra - spread * later)
        ceiling = jnp.minimum(spread, extra)
        portion = jax.random.randint(split_keys[clip], (pairs,), floor_part, ceiling + 1, dtype=jnp.int32)
        shares.append(portion)
        extra = extra - portion
    shares.append(extra)
    second = lowest + jnp.stack(shares, axis=1)
    flip = jax.random.randint(order_key, (pairs, 1), 0, 2, dtype=jnp.int32)
    block_even = jnp.where(flip == 0, first, second)
    block_odd = jnp.where(flip == 0, second, first)
    return jnp.stack([block_even, block_odd], axis=1).reshape(-1).astype(jnp.int32)


def draw_clip_counts(key, part):
    return pair_counts(key)


def draw_tube_index(key, part):
    blocks = N_FSDP * N_DP
    counts = pair_counts(key).reshape(blocks, CLIP_DEV)
    key = jax.random.fold_in(key, 7)
    tubes = TSTEPS * GRID * GRID
    clip_keys = jax.random.split(key, blocks * CLIP_DEV)

    def choose(clip_key):
        return jax.random.permutation(clip_key, tubes)[:CAP]
    chosen = jax.vmap(choose)(clip_keys).reshape(blocks, CLIP_DEV, CAP).astype(jnp.int32)
    slot = jnp.arange(CAP)
    chosen = jnp.where(slot[None, None, :] < counts[:, :, None], chosen, 2 * tubes)
    chosen = jnp.sort(chosen, axis=2)
    bounds = jnp.cumsum(counts, axis=1)
    starts = bounds - counts
    place = jnp.arange(ROWS_DEV)
    clip_of = jnp.sum((place[None, :, None] >= bounds[:, None, :]).astype(jnp.int32), axis=2)
    clamped = jnp.minimum(clip_of, CLIP_DEV - 1)
    start_of = jnp.take_along_axis(starts, clamped, axis=1)
    within = jnp.clip(place[None, :] - start_of, 0, CAP - 1)
    flat = chosen.reshape(blocks, CLIP_DEV * CAP)
    picked = jnp.take_along_axis(flat, clamped * CAP + within, axis=1)
    return jnp.where(clip_of < CLIP_DEV, picked, 0).astype(jnp.int32).reshape(-1)


def draw_projected(key, part):
    key = jax.random.fold_in(key, 11)
    shape = (ROWS, 3 * HD)
    base_key = jax.random.fold_in(key, 0)
    return jnp.clip(jax.random.normal(base_key, shape, jnp.float32), -6.0, 6.0).astype(jnp.bfloat16)


def block_scale(rng, extent, cuts, smallest, top_value):
    def one(position, shards_of):
        steps = jax.random.uniform(jax.random.fold_in(jax.random.fold_in(rng, 6), position), (shards_of,), jnp.float32, smallest / len(cuts), top_value / len(cuts))
        return jnp.repeat(jnp.exp(steps), extent[position] // shards_of).reshape((-1,) + (1,) * (len(extent) - position - 1))

    level = one(*cuts[0])
    for cut in cuts[1:]:
        level = level * one(*cut)
    return level


def noise(own_key, dims, width, reach, shards=(), held_as=jnp.bfloat16):
    gain = block_scale(own_key, dims, shards, -0.22, 0.18) if shards else 1.0
    array = jax.random.normal(own_key, dims, jnp.float32) * width * gain
    return jnp.minimum(jnp.maximum(array, -reach), reach).astype(held_as)


def setup_inputs(seed: int = 0) -> dict:
    key_list = jax.random.split(jax.random.key(seed), 6)
    projected = draw_projected(jax.random.fold_in(key_list[5], 71), 0)
    cotangent = noise(key_list[1], (ROWS, D), 1.0, 6.0, ((0, 32),))
    out_weight = noise(key_list[2], (HD, D), HD ** -0.5, 0.15625, ((0, 16),), jnp.float32)
    clip_counts = draw_clip_counts(jax.random.fold_in(key_list[5], 71), 0)
    tube_index = draw_tube_index(jax.random.fold_in(key_list[5], 71), 0)
    return dict(projected=projected, cotangent=cotangent, out_weight=out_weight, clip_counts=clip_counts, tube_index=tube_index)


HALF = 64


def pair_table():
    index = np.arange(HALF)
    first = index < 16
    second = (index >= 16) & (index < 40)
    exponent = np.where(first, index / 16.0, np.where(second, (index - 16) / 24.0, (index - 40) / 24.0))
    which = np.where(first, 0, np.where(second, 1, 2))
    return 100.0 ** (-exponent), which


def angles(tube_index):
    frequency, which = pair_table()
    temporal = tube_index // (GRID * GRID)
    vertical = (tube_index // GRID) % GRID
    lateral = tube_index % GRID
    coords = jnp.stack([temporal, vertical, lateral], axis=1).astype(jnp.float32)
    angle = coords[:, which] * jnp.asarray(frequency, dtype=jnp.float32)[None, :]
    return jnp.cos(angle)[:, None, :], jnp.sin(angle)[:, None, :]


def rotate(values, cosine, sine):
    first = values[..., :HALF].astype(jnp.float32)
    second = values[..., HALF:].astype(jnp.float32)
    return jnp.concatenate([first * cosine - second * sine, second * cosine + first * sine], axis=-1)


def unrotate(grads, cosine, sine):
    first = grads[..., :HALF]
    second = grads[..., HALF:]
    return jnp.concatenate([first * cosine + second * sine, second * cosine - first * sine], axis=-1)


def softmax_rows(query_one, keys_one, same_clip, scale):
    scores = jnp.dot(query_one, keys_one.T, preferred_element_type=jnp.float32) * scale
    scores = jnp.where(same_clip, scores, -1e30)
    row_top = jnp.max(scores, axis=1, keepdims=True)
    lifted = jnp.exp(scores - row_top)
    return lifted / jnp.sum(lifted, axis=1, keepdims=True)


def block_terms(projected, cotangent, tube_index, clip_counts, weight_copy):
    row_count = projected.shape[0]
    scale = HS ** -0.5
    bounds = jnp.cumsum(clip_counts)
    place = jnp.arange(row_count)
    clip_of = jnp.sum((place[:, None] >= bounds[None, :]).astype(jnp.int32), axis=1)
    live = clip_of < CLIP_DEV
    same_clip = clip_of[:, None] == clip_of[None, :]
    live_float = live.astype(jnp.float32)
    live_rows = live.astype(jnp.bfloat16)[:, None]
    cosine, sine = angles(tube_index)
    query = rotate(projected[:, :HD].reshape(row_count, H, HS), cosine, sine).astype(jnp.bfloat16)
    keys = rotate(projected[:, HD:2 * HD].reshape(row_count, H, HS), cosine, sine).astype(jnp.bfloat16)
    values = projected[:, 2 * HD:].reshape(row_count, H, HS)
    query_heads = jnp.swapaxes(query, 0, 1)
    keys_heads = jnp.swapaxes(keys, 0, 1)
    values_heads = jnp.swapaxes(values, 0, 1)

    def head_forward(operands):
        query_one, keys_one, values_one = operands
        probs = softmax_rows(query_one, keys_one, same_clip, scale)
        mixed = jnp.dot(probs.astype(jnp.bfloat16), values_one, preferred_element_type=jnp.float32)
        return (mixed * live_float[:, None]).astype(jnp.bfloat16)

    attn = jnp.swapaxes(lax.map(head_forward, (query_heads, keys_heads, values_heads)), 0, 1).reshape(row_count, HD)
    out_rows = jnp.dot(attn, weight_copy, preferred_element_type=jnp.float32).astype(jnp.bfloat16)
    masked_cot = cotangent * live_rows
    grad_attn = jnp.dot(masked_cot, weight_copy.T, preferred_element_type=jnp.float32).astype(jnp.bfloat16)
    weight_term = jnp.dot(attn.T, masked_cot, preferred_element_type=jnp.float32)
    grad_heads = jnp.swapaxes(grad_attn.reshape(row_count, H, HS), 0, 1)

    def head_backward(operands):
        query_one, keys_one, values_one, grad_one = operands
        probs = softmax_rows(query_one, keys_one, same_clip, scale)
        probs_low = probs.astype(jnp.bfloat16)
        grad_values = jnp.dot(probs_low.T, grad_one, preferred_element_type=jnp.float32).astype(jnp.bfloat16)
        grad_probs = jnp.dot(grad_one, values_one.T, preferred_element_type=jnp.float32)
        centre = jnp.sum(probs * grad_probs, axis=1, keepdims=True)
        grad_scores = (probs * (grad_probs - centre) * scale).astype(jnp.bfloat16)
        grad_query = jnp.dot(grad_scores, keys_one, preferred_element_type=jnp.float32)
        grad_keys = jnp.dot(grad_scores.T, query_one, preferred_element_type=jnp.float32)
        return grad_query, grad_keys, grad_values

    grad_query, grad_keys, grad_values = lax.map(head_backward, (query_heads, keys_heads, values_heads, grad_heads))
    grad_query = unrotate(jnp.swapaxes(grad_query, 0, 1), cosine, sine).astype(jnp.bfloat16).reshape(row_count, HD)
    grad_keys = unrotate(jnp.swapaxes(grad_keys, 0, 1), cosine, sine).astype(jnp.bfloat16).reshape(row_count, HD)
    grad_values = jnp.swapaxes(grad_values, 0, 1).reshape(row_count, HD)
    grad_projected = jnp.concatenate([grad_query, grad_keys, grad_values], axis=1)
    return out_rows, grad_projected, weight_term


def reference(projected, cotangent, out_weight, clip_counts, tube_index):
    blocks = N_FSDP * N_DP
    weight_copy = out_weight.astype(jnp.bfloat16)
    stacked = (
        projected.reshape(blocks, ROWS_DEV, 3 * HD),
        cotangent.reshape(blocks, ROWS_DEV, D),
        tube_index.reshape(blocks, ROWS_DEV),
        clip_counts.reshape(blocks, CLIP_DEV),
    )

    def step(total, block):
        out_rows, grad_projected, weight_term = block_terms(block[0], block[1], block[2], block[3], weight_copy)
        return total + weight_term, (out_rows, grad_projected)

    total, (outputs, grads) = lax.scan(step, jnp.zeros((HD, D), jnp.float32), stacked)
    return outputs.reshape(ROWS, D), grads.reshape(ROWS, 3 * HD), total
```

```python
import jax
import jax.numpy as jnp
import numpy as np
from jax import lax
from jax.experimental import pallas as pl
from jax.experimental.pallas import tpu as pltpu
from jax.sharding import PartitionSpec as P

HS = 128
GRID = 16
HALF = 64
CHUNKS = 5
NEG = -1e30
VMEM_BYTES = 48 * 1024 * 1024


def pair_table():
    index = np.arange(HALF)
    first = index < 16
    second = (index >= 16) & (index < 40)
    exponent = np.where(
        first, index / 16.0, np.where(second, (index - 16) / 24.0, (index - 40) / 24.0)
    )
    which = np.where(first, 0, np.where(second, 1, 2))
    return (100.0 ** (-exponent), which)


def angles(tube_index):
    frequency, which = pair_table()
    temporal = (tube_index // (GRID * GRID)).astype(jnp.float32)[:, None]
    vertical = (tube_index // GRID % GRID).astype(jnp.float32)[:, None]
    lateral = (tube_index % GRID).astype(jnp.float32)[:, None]
    which = jnp.asarray(which)[None, :]
    coords = jnp.where(which == 0, temporal, jnp.where(which == 1, vertical, lateral))
    angle = coords * jnp.asarray(frequency, dtype=jnp.float32)[None, :]
    cosine, sine = jnp.cos(angle), jnp.sin(angle)
    return (
        jnp.concatenate([cosine, cosine], axis=1),
        jnp.concatenate([-sine, sine], axis=1),
    )


def rotate(values, cosine, sine):
    wide = values.astype(jnp.float32)
    return wide * cosine + pltpu.roll(wide, HALF, 1) * sine


def unrotate(grads, cosine, sine):
    return grads * cosine - pltpu.roll(grads, HALF, 1) * sine


def windows(counts_ref, rows):
    first, second = counts_ref[0], counts_ref[1]
    half = rows // 2
    wide = half + 16
    start = jnp.minimum(first // 16 * 16, rows - wide)
    return (
        (0, half, 0, first),
        (pl.multiple_of(start, 16), wide, first, first + second),
    )


def probs_t(keys, query, start, low, high, scale):
    scores = (
        lax.dot_general(
            keys, query, (((1,), (1,)), ((), ())), preferred_element_type=jnp.float32
        )
        * scale
    )
    place = start + lax.broadcasted_iota(jnp.int32, (keys.shape[0], 1), 0)
    scores = jnp.where((place >= low) & (place < high), scores, NEG)
    lifted = jnp.exp(scores - jnp.max(scores, axis=0, keepdims=True))
    return lifted * (1.0 / jnp.sum(lifted, axis=0, keepdims=True))


def forward_kernel(
    counts_ref, q_ref, k_ref, v_ref, cos_ref, sin_ref, out_ref, qr, kr, total
):
    rows = q_ref.shape[0]
    scale = HS ** (-0.5)
    cosine, sine = cos_ref[...], sin_ref[...]
    qr[...] = rotate(q_ref[...], cosine, sine).astype(jnp.bfloat16)
    kr[...] = rotate(k_ref[...], cosine, sine).astype(jnp.bfloat16)
    total[...] = jnp.zeros_like(total)
    for start, wide, low, high in windows(counts_ref, rows):
        span = pl.ds(start, wide)
        probs = probs_t(kr[span, :], qr[span, :], start, low, high, scale)
        mixed = lax.dot_general(
            v_ref[span, :],
            probs.astype(jnp.bfloat16),
            (((0,), (0,)), ((), ())),
            preferred_element_type=jnp.float32,
        ).T
        place = start + lax.broadcasted_iota(jnp.int32, (wide, 1), 0)
        total[span, :] += jnp.where((place >= low) & (place < high), mixed, 0.0)
    out_ref[...] = total[...].T.astype(jnp.bfloat16)


def backward_kernel(
    counts_ref, q_ref, k_ref, v_ref, g_ref, cos_ref, sin_ref, out_ref, qr, kr, go, total, low_out
):
    part = pl.program_id(1)

    @pl.when(part == 0)
    def _():
        rows = q_ref.shape[0]
        scale = HS ** (-0.5)
        cosine, sine = cos_ref[...], sin_ref[...]
        qr[...] = rotate(q_ref[...], cosine, sine).astype(jnp.bfloat16)
        kr[...] = rotate(k_ref[...], cosine, sine).astype(jnp.bfloat16)
        go[...] = g_ref[...].astype(jnp.float32).T.astype(jnp.bfloat16)
        total[...] = jnp.zeros_like(total)
        for start, wide, low, high in windows(counts_ref, rows):
            span = pl.ds(start, wide)
            keys, query, values = kr[span, :], qr[span, :], v_ref[span, :]
            place = start + lax.broadcasted_iota(jnp.int32, (wide, 1), 0)
            grad = jnp.where(
                (place >= low) & (place < high), go[span, :].astype(jnp.float32), 0.0
            ).astype(jnp.bfloat16)
            probs = probs_t(keys, query, start, low, high, scale)
            total[2, span, :] += jnp.dot(
                probs.astype(jnp.bfloat16), grad, preferred_element_type=jnp.float32
            )
            grad_probs = lax.dot_general(
                values, grad, (((1,), (1,)), ((), ())), preferred_element_type=jnp.float32
            )
            centre = jnp.sum(probs * grad_probs, axis=0, keepdims=True)
            grad_scores = (probs * (grad_probs - centre) * scale).astype(jnp.bfloat16)
            total[1, span, :] += jnp.dot(grad_scores, query, preferred_element_type=jnp.float32)
            total[0, span, :] += lax.dot_general(
                keys, grad_scores, (((0,), (0,)), ((), ())), preferred_element_type=jnp.float32
            ).T
        low_out[0] = unrotate(total[0], cosine, sine).astype(jnp.bfloat16)
        low_out[1] = unrotate(total[1], cosine, sine).astype(jnp.bfloat16)
        low_out[2] = total[2].astype(jnp.bfloat16)

    out_ref[...] = low_out[part]


def attention_forward(projected, clip_counts, cosine, sine):
    rows = projected.shape[0]
    heads = projected.shape[1] // 3 // HS
    whole = pl.BlockSpec((rows, HS), lambda h, c: (0, 0))
    return pl.pallas_call(
        forward_kernel,
        grid_spec=pltpu.PrefetchScalarGridSpec(
            num_scalar_prefetch=1,
            grid=(heads,),
            in_specs=[
                pl.BlockSpec((rows, HS), lambda h, c: (0, h)),
                pl.BlockSpec((rows, HS), lambda h, c: (0, h + heads)),
                pl.BlockSpec((rows, HS), lambda h, c: (0, h + 2 * heads)),
                whole,
                whole,
            ],
            out_specs=pl.BlockSpec((HS, rows), lambda h, c: (h, 0)),
            scratch_shapes=[
                pltpu.VMEM((rows, HS), jnp.bfloat16),
                pltpu.VMEM((rows, HS), jnp.bfloat16),
                pltpu.VMEM((rows, HS), jnp.float32),
            ],
        ),
        out_shape=jax.ShapeDtypeStruct((heads * HS, rows), jnp.bfloat16),
        compiler_params=pltpu.CompilerParams(vmem_limit_bytes=VMEM_BYTES),
        cost_estimate=pl.CostEstimate(
            flops=heads * rows * rows * HS * 6, bytes_accessed=rows * heads * HS * 8,
            transcendentals=heads * rows * rows,
        ),
    )(clip_counts, projected, projected, projected, cosine, sine)


def attention_backward(projected, clip_counts, grad_t, cosine, sine):
    rows = projected.shape[0]
    heads = projected.shape[1] // 3 // HS
    whole = pl.BlockSpec((rows, HS), lambda h, j, c: (0, 0))
    return pl.pallas_call(
        backward_kernel,
        grid_spec=pltpu.PrefetchScalarGridSpec(
            num_scalar_prefetch=1,
            grid=(heads, 3),
            in_specs=[
                pl.BlockSpec((rows, HS), lambda h, j, c: (0, h)),
                pl.BlockSpec((rows, HS), lambda h, j, c: (0, h + heads)),
                pl.BlockSpec((rows, HS), lambda h, j, c: (0, h + 2 * heads)),
                pl.BlockSpec((HS, rows), lambda h, j, c: (h, 0)),
                whole,
                whole,
            ],
            out_specs=pl.BlockSpec((rows, HS), lambda h, j, c: (0, j * heads + h)),
            scratch_shapes=[
                pltpu.VMEM((rows, HS), jnp.bfloat16),
                pltpu.VMEM((rows, HS), jnp.bfloat16),
                pltpu.VMEM((rows, HS), jnp.bfloat16),
                pltpu.VMEM((3, rows, HS), jnp.float32),
                pltpu.VMEM((3, rows, HS), jnp.bfloat16),
            ],
        ),
        out_shape=jax.ShapeDtypeStruct(projected.shape, jnp.bfloat16),
        compiler_params=pltpu.CompilerParams(vmem_limit_bytes=VMEM_BYTES),
        cost_estimate=pl.CostEstimate(
            flops=heads * rows * rows * HS * 14, bytes_accessed=rows * heads * HS * 14,
            transcendentals=heads * rows * rows,
        ),
    )(clip_counts, projected, projected, projected, grad_t, cosine, sine)


def body(sizes, projected, cotangent, out_weight, clip_counts, tube_index):
    devices, pair = sizes
    bits = devices.bit_length() - 1
    rows = projected.shape[0]
    head_width = projected.shape[1] // 3
    depth = out_weight.shape[0]
    width = out_weight.shape[1]
    piece = width // CHUNKS
    me = lax.axis_index("fsdp")
    row_side = lax.axis_index("dp")

    def across(array, bit):
        if bit < 0:
            return lax.ppermute(array, "dp", [(i, i ^ 1) for i in range(pair)])
        return lax.ppermute(array, "fsdp", [(i, i ^ (1 << bit)) for i in range(devices)])

    slot = np.array([int(format(i, f"0{bits}b")[::-1], 2) for i in range(devices)])

    def to_places(array):
        return jnp.concatenate(
            [
                lax.dynamic_slice_in_dim(array, (int(p) ^ me) * depth, depth, 0)
                for p in slot
            ],
            axis=0,
        )

    def from_places(array):
        table = jnp.asarray(slot, dtype=jnp.int32)
        return jnp.concatenate(
            [
                lax.dynamic_slice_in_dim(array, table[j ^ me] * depth, depth, 0)
                for j in range(devices)
            ],
            axis=0,
        )

    x_bit, z_bits = 1, list(range(2, bits))

    def gather(part, order):
        array = part.reshape((1,) * bits + part.shape)
        for bit in order:
            array = jnp.concatenate([array, across(array, bit)], axis=bit)
        return array.reshape(devices * depth, piece)

    def reduce(keep, send, order):
        array = keep + across(send, 0)
        array = array.reshape((1,) + (2,) * (bits - 1) + (depth, piece))
        for bit in order:
            if bit < 0:
                continue
            send = lax.slice_in_dim(array, 1, 2, axis=bit)
            keep = lax.slice_in_dim(array, 0, 1, axis=bit)
            array = keep + across(send, bit)
        return array.reshape(depth, piece)

    weight_copy = out_weight.astype(jnp.bfloat16)

    def columns(array, index):
        return lax.dynamic_slice_in_dim(array, index * piece, piece, 1)

    down = z_bits[::-1]
    own = gather(columns(weight_copy, row_side), [x_bit] + down + [0])
    other = across(own, -1)
    weights = [jnp.where(row_side == 0, own, other), jnp.where(row_side == 0, other, own)]
    for index in (2, 3):
        weights.append(gather(columns(weight_copy, index), down + [x_bit, 0]))
    weights.append(gather(columns(weight_copy, 4), [x_bit] + down + [0]))
    full_weight = jnp.concatenate(weights, axis=1)

    bounds = jnp.cumsum(clip_counts)
    live_rows = (jnp.arange(rows) < bounds[-1]).astype(jnp.bfloat16)[:, None]
    cosine, sine = angles(tube_index)
    masked_cot = cotangent * live_rows
    attn_t = to_places(attention_forward(projected, clip_counts, cosine, sine))
    half = head_width // 2
    keep_t, send_t = attn_t[:half], attn_t[half:]

    def product(left, index):
        return jnp.dot(left, columns(masked_cot, index), preferred_element_type=jnp.float32)

    mine, theirs = row_side, 1 - row_side
    own_keep, own_send = product(keep_t, mine), product(send_t, mine)
    other_keep, other_send = product(keep_t, theirs), product(send_t, theirs)
    pair_send = other_keep + across(other_send, 0)
    pair_keep = own_keep + across(own_send, 0)
    array = pair_keep + across(pair_send, -1)
    array = array.reshape((1,) + (2,) * (bits - 1) + (depth, piece))
    for bit in z_bits + [x_bit]:
        array = lax.slice_in_dim(array, 0, 1, axis=bit) + across(
            lax.slice_in_dim(array, 1, 2, axis=bit), bit
        )
    own = array.reshape(depth, piece)
    other = across(own, -1)
    grads = [jnp.where(row_side == 0, own, other), jnp.where(row_side == 0, other, own)]
    for index, order in ((2, [x_bit] + z_bits), (3, [x_bit] + z_bits), (4, z_bits + [x_bit])):
        own = reduce(product(keep_t, index), product(send_t, index), order)
        grads.append(own + across(own, -1))
    grad_weight = jnp.concatenate(grads, axis=1)

    grad_t = lax.dot_general(
        full_weight, masked_cot, (((1,), (1,)), ((), ())), preferred_element_type=jnp.float32
    ).astype(jnp.bfloat16)
    grad_projected = attention_backward(
        projected, clip_counts, from_places(grad_t), cosine, sine
    )
    work_out = lax.dot_general(
        attn_t, full_weight, (((0,), (0,)), ((), ())), preferred_element_type=jnp.float32
    ).astype(jnp.bfloat16)
    return (work_out, grad_projected, grad_weight)


def solution(mesh):
    placed = (
        P(("fsdp", "dp"), None),
        P(("fsdp", "dp"), None),
        P("fsdp", None),
        P(("fsdp", "dp")),
        P(("fsdp", "dp")),
    )
    sizes = (mesh.shape["fsdp"], mesh.shape["dp"])

    def local(*args):
        return body(sizes, *args)

    return jax.shard_map(
        local,
        mesh=mesh,
        in_specs=placed,
        out_specs=(P(("fsdp", "dp"), None), P(("fsdp", "dp"), None), P("fsdp", None)),
        check_vma=False,
    )
```

```python
import jax
import jax.numpy as jnp
import numpy as np
from jax import lax
from jax.experimental import pallas as pl
from jax.experimental.pallas import tpu as pltpu
from jax.sharding import PartitionSpec as P

HS = 128
GRID = 16
HALF = 64
CHUNKS = 5
NEG = -1e30
VMEM_BYTES = 48 * 1024 * 1024


def pair_table():
    index = np.arange(HALF)
    first = index < 16
    second = (index >= 16) & (index < 40)
    exponent = np.where(
        first, index / 16.0, np.where(second, (index - 16) / 24.0, (index - 40) / 24.0)
    )
    which = np.where(first, 0, np.where(second, 1, 2))
    return (100.0 ** (-exponent), which)


def angles(tube_index):
    frequency, which = pair_table()
    temporal = (tube_index // (GRID * GRID)).astype(jnp.float32)[:, None]
    vertical = (tube_index // GRID % GRID).astype(jnp.float32)[:, None]
    lateral = (tube_index % GRID).astype(jnp.float32)[:, None]
    which = jnp.asarray(which)[None, :]
    coords = jnp.where(which == 0, temporal, jnp.where(which == 1, vertical, lateral))
    angle = coords * jnp.asarray(frequency, dtype=jnp.float32)[None, :]
    cosine, sine = jnp.cos(angle), jnp.sin(angle)
    return (
        jnp.concatenate([cosine, cosine], axis=1),
        jnp.concatenate([-sine, sine], axis=1),
    )


def rotate(values, cosine, sine):
    wide = values.astype(jnp.float32)
    return wide * cosine + pltpu.roll(wide, HALF, 1) * sine


def unrotate(grads, cosine, sine):
    return grads * cosine - pltpu.roll(grads, HALF, 1) * sine


def windows(counts_ref, rows):
    first, second = counts_ref[0], counts_ref[1]
    half = rows // 2
    wide = half + 16
    start = jnp.minimum(first // 16 * 16, rows - wide)
    return (
        (0, half, 0, first),
        (pl.multiple_of(start, 16), wide, first, first + second),
    )


def probs_t(keys, query, start, low, high, scale):
    scores = (
        lax.dot_general(
            keys, query, (((1,), (1,)), ((), ())), preferred_element_type=jnp.float32
        )
        * scale
    )
    place = start + lax.broadcasted_iota(jnp.int32, (keys.shape[0], 1), 0)
    scores = jnp.where((place >= low) & (place < high), scores, NEG)
    lifted = jnp.exp(scores - jnp.max(scores, axis=0, keepdims=True))
    return lifted * (1.0 / jnp.sum(lifted, axis=0, keepdims=True))


def forward_kernel(
    counts_ref, q_ref, k_ref, v_ref, cos_ref, sin_ref, out_ref, qr, kr, total
):
    rows = q_ref.shape[0]
    scale = HS ** (-0.5)
    cosine, sine = cos_ref[...], sin_ref[...]
    qr[...] = rotate(q_ref[...], cosine, sine).astype(jnp.bfloat16)
    kr[...] = rotate(k_ref[...], cosine, sine).astype(jnp.bfloat16)
    total[...] = jnp.zeros_like(total)
    for start, wide, low, high in windows(counts_ref, rows):
        span = pl.ds(start, wide)
        probs = probs_t(kr[span, :], qr[span, :], start, low, high, scale)
        mixed = lax.dot_general(
            v_ref[span, :],
            probs.astype(jnp.bfloat16),
            (((0,), (0,)), ((), ())),
            preferred_element_type=jnp.float32,
        ).T
        place = start + lax.broadcasted_iota(jnp.int32, (wide, 1), 0)
        total[span, :] += jnp.where((place >= low) & (place < high), mixed, 0.0)
    out_ref[...] = total[...].T.astype(jnp.bfloat16)


def backward_kernel(
    counts_ref, q_ref, k_ref, v_ref, g_ref, cos_ref, sin_ref, out_ref, qr, kr, go, total, low_out
):
    part = pl.program_id(1)

    @pl.when(part == 0)
    def _():
        rows = q_ref.shape[0]
        scale = HS ** (-0.5)
        cosine, sine = cos_ref[...], sin_ref[...]
        qr[...] = rotate(q_ref[...], cosine, sine).astype(jnp.bfloat16)
        kr[...] = rotate(k_ref[...], cosine, sine).astype(jnp.bfloat16)
        go[...] = g_ref[...].astype(jnp.float32).T.astype(jnp.bfloat16)
        total[...] = jnp.zeros_like(total)
        for start, wide, low, high in windows(counts_ref, rows):
            span = pl.ds(start, wide)
            keys, query, values = kr[span, :], qr[span, :], v_ref[span, :]
            place = start + lax.broadcasted_iota(jnp.int32, (wide, 1), 0)
            grad = jnp.where(
                (place >= low) & (place < high), go[span, :].astype(jnp.float32), 0.0
            ).astype(jnp.bfloat16)
            probs = probs_t(keys, query, start, low, high, scale)
            total[2, span, :] += jnp.dot(
                probs.astype(jnp.bfloat16), grad, preferred_element_type=jnp.float32
            )
            grad_probs = lax.dot_general(
                values, grad, (((1,), (1,)), ((), ())), preferred_element_type=jnp.float32
            )
            centre = jnp.sum(probs * grad_probs, axis=0, keepdims=True)
            grad_scores = (probs * (grad_probs - centre) * scale).astype(jnp.bfloat16)
            total[1, span, :] += jnp.dot(grad_scores, query, preferred_element_type=jnp.float32)
            total[0, span, :] += lax.dot_general(
                keys, grad_scores, (((0,), (0,)), ((), ())), preferred_element_type=jnp.float32
            ).T
        low_out[0] = unrotate(total[0], cosine, sine).astype(jnp.bfloat16)
        low_out[1] = unrotate(total[1], cosine, sine).astype(jnp.bfloat16)
        low_out[2] = total[2].astype(jnp.bfloat16)

    out_ref[...] = low_out[part]


def attention_forward(projected, clip_counts, cosine, sine):
    rows = projected.shape[0]
    heads = projected.shape[1] // 3 // HS
    whole = pl.BlockSpec((rows, HS), lambda h, c: (0, 0))
    return pl.pallas_call(
        forward_kernel,
        grid_spec=pltpu.PrefetchScalarGridSpec(
            num_scalar_prefetch=1,
            grid=(heads,),
            in_specs=[
                pl.BlockSpec((rows, HS), lambda h, c: (0, h)),
                pl.BlockSpec((rows, HS), lambda h, c: (0, h + heads)),
                pl.BlockSpec((rows, HS), lambda h, c: (0, h + 2 * heads)),
                whole,
                whole,
            ],
            out_specs=pl.BlockSpec((HS, rows), lambda h, c: (h, 0)),
            scratch_shapes=[
                pltpu.VMEM((rows, HS), jnp.bfloat16),
                pltpu.VMEM((rows, HS), jnp.bfloat16),
                pltpu.VMEM((rows, HS), jnp.float32),
            ],
        ),
        out_shape=jax.ShapeDtypeStruct((heads * HS, rows), jnp.bfloat16),
        compiler_params=pltpu.CompilerParams(vmem_limit_bytes=VMEM_BYTES),
        cost_estimate=pl.CostEstimate(
            flops=heads * rows * rows * HS * 6, bytes_accessed=rows * heads * HS * 8,
            transcendentals=heads * rows * rows,
        ),
    )(clip_counts, projected, projected, projected, cosine, sine)


def attention_backward(projected, clip_counts, grad_t, cosine, sine, heads_from, heads_to, before):
    rows = projected.shape[0]
    heads = projected.shape[1] // 3 // HS
    count = heads_to - heads_from
    whole = pl.BlockSpec((rows, HS), lambda h, j, c: (0, 0))
    at = heads_from
    in_specs = [
        pl.BlockSpec((rows, HS), lambda h, j, c: (0, at + h)),
        pl.BlockSpec((rows, HS), lambda h, j, c: (0, at + h + heads)),
        pl.BlockSpec((rows, HS), lambda h, j, c: (0, at + h + 2 * heads)),
        pl.BlockSpec((HS, rows), lambda h, j, c: (at + h, 0)),
        whole,
        whole,
    ]
    operands = [clip_counts, projected, projected, projected, grad_t, cosine, sine]
    kernel, aliases = backward_kernel, {}
    if before is not None:
        in_specs.append(pl.BlockSpec(memory_space=pl.ANY))
        aliases = {len(operands): 0}
        operands.append(before)

        def kernel(*refs):
            backward_kernel(*refs[:7], *refs[8:])

    return pl.pallas_call(
        kernel,
        grid_spec=pltpu.PrefetchScalarGridSpec(
            num_scalar_prefetch=1,
            grid=(count, 3),
            in_specs=in_specs,
            out_specs=pl.BlockSpec((rows, HS), lambda h, j, c: (0, j * heads + at + h)),
            scratch_shapes=[
                pltpu.VMEM((rows, HS), jnp.bfloat16),
                pltpu.VMEM((rows, HS), jnp.bfloat16),
                pltpu.VMEM((rows, HS), jnp.bfloat16),
                pltpu.VMEM((3, rows, HS), jnp.float32),
                pltpu.VMEM((3, rows, HS), jnp.bfloat16),
            ],
        ),
        out_shape=jax.ShapeDtypeStruct(projected.shape, jnp.bfloat16),
        input_output_aliases=aliases,
        compiler_params=pltpu.CompilerParams(vmem_limit_bytes=VMEM_BYTES),
        cost_estimate=pl.CostEstimate(
            flops=count * rows * rows * HS * 70, bytes_accessed=rows * count * HS * 14,
            transcendentals=count * rows * rows,
        ),
    )(*operands)


def body(sizes, projected, cotangent, out_weight, clip_counts, tube_index):
    devices, pair = sizes
    bits = devices.bit_length() - 1
    rows = projected.shape[0]
    head_width = projected.shape[1] // 3
    heads = head_width // HS
    depth = out_weight.shape[0]
    width = out_weight.shape[1]
    piece = width // CHUNKS
    me = lax.axis_index("fsdp")
    row_side = lax.axis_index("dp")

    def across(array, bit):
        if bit < 0:
            return lax.ppermute(array, "dp", [(i, i ^ 1) for i in range(pair)])
        return lax.ppermute(array, "fsdp", [(i, i ^ (1 << bit)) for i in range(devices)])

    slot_of = [int(format(i, f"0{bits}b")[::-1], 2) for i in range(devices)]

    def to_places(array):
        return jnp.concatenate(
            [lax.dynamic_slice_in_dim(array, (p ^ me) * depth, depth, 0) for p in slot_of],
            axis=0,
        )

    def part_of(array, bit, which):
        return lax.slice_in_dim(array, which, which + 1, axis=bit)

    def together(sends, work_in, work):
        arrays, work_in = lax.optimization_barrier(([a for a, _ in sends], work_in))
        arrived = [across(a, bit) for a, (_, bit) in zip(arrays, sends)]
        return lax.optimization_barrier((arrived, work(work_in)))

    full_weight = lax.all_gather(out_weight.astype(jnp.bfloat16), "fsdp", axis=0, tiled=True)
    bounds = jnp.cumsum(clip_counts)
    live_rows = (jnp.arange(rows) < bounds[-1]).astype(jnp.bfloat16)[:, None]
    cosine, sine = angles(tube_index)
    masked_cot = cotangent * live_rows
    attn_t = attention_forward(projected, clip_counts, cosine, sine)
    placed_t = to_places(attn_t)
    half = head_width // 2
    keep_t, send_t = placed_t[:half], placed_t[half:]
    cubes = (1,) + (2,) * (bits - 1) + (depth, piece)

    def product(left, index):
        cot = lax.dynamic_slice_in_dim(masked_cot, index * piece, piece, 1)
        return jnp.dot(left, cot, preferred_element_type=jnp.float32)

    def first_sum(index):
        sent = across(product(send_t, index), 0)
        return (product(keep_t, index) + sent).reshape(cubes)

    x, near, far = 1, 2, list(range(3, bits))
    last = far[-1] if far else None
    give = first_sum(1 - row_side)
    second = first_sum(2)
    fifth = first_sum(4)
    own = first_sum(row_side)
    third = first_sum(3)

    def nothing(value):
        return value

    def step(array, bit):
        return part_of(array, bit, 0), part_of(array, bit, 1)

    def middle(array):
        for bit in far[:-1]:
            low, high = step(array, bit)
            array = low + across(high, bit)
        return array

    (g_in, s_in, f_in), _ = together(
        [(part_of(give, near, 1), -1), (part_of(second, x, 1), x), (part_of(fifth, near, 1), near)],
        (),
        nothing,
    )
    ahead = part_of(own, near, 1) + g_in
    second = part_of(second, x, 0) + s_in
    fifth = middle(part_of(fifth, near, 0) + f_in)
    (g_in, a_in, t_in, f_in), _ = together(
        [
            (part_of(give, near, 0), -1),
            (ahead, near),
            (part_of(third, x, 1), x),
            (part_of(fifth, last, 1), last),
        ],
        (),
        nothing,
    )
    own = middle(part_of(own, near, 0) + g_in + a_in)
    third = part_of(third, x, 0) + t_in
    fifth = part_of(fifth, last, 0) + f_in

    def grad_of(weight):
        return lax.dot_general(
            weight, masked_cot, (((1,), (1,)), ((), ())), preferred_element_type=jnp.float32
        ).astype(jnp.bfloat16)

    cuts = (0, heads * 2 // 13, heads * 8 // 13, heads)

    def backward(grad_t, index, before):
        return attention_backward(
            projected, clip_counts, grad_t, cosine, sine, cuts[index], cuts[index + 1], before
        )

    def work_one(weight):
        grad_t = grad_of(weight)
        return grad_t, backward(grad_t, 0, None)

    (o_in, s_in, t_in, f_in), (grad_t, grad_projected) = together(
        [
            (part_of(own, last, 1), last),
            (part_of(second, near, 1), near),
            (part_of(third, near, 1), near),
            (part_of(fifth, x, 1), x),
        ],
        full_weight,
        work_one,
    )
    own = part_of(own, last, 0) + o_in
    second = middle(part_of(second, near, 0) + s_in)
    third = middle(part_of(third, near, 0) + t_in)
    fifth = part_of(fifth, x, 0) + f_in
    (o_in, s_in, t_in, f_in), (grad_t, grad_projected) = together(
        [
            (part_of(own, x, 1), x),
            (part_of(second, last, 1), last),
            (part_of(third, last, 1), last),
            (fifth, -1),
        ],
        (grad_t, grad_projected),
        lambda held: (held[0], backward(held[0], 1, held[1])),
    )
    own = part_of(own, x, 0) + o_in
    second = part_of(second, last, 0) + s_in
    third = part_of(third, last, 0) + t_in
    fifth = fifth + f_in

    def work_last(held):
        grad_t, grad_projected = held
        out = lax.dot_general(
            attn_t, full_weight, (((0,), (0,)), ((), ())), preferred_element_type=jnp.float32
        ).astype(jnp.bfloat16)
        return out, backward(grad_t, 2, grad_projected)

    (o_in, s_in, t_in), (work_out, grad_projected) = together(
        [(own, -1), (second, -1), (third, -1)], (grad_t, grad_projected), work_last
    )
    pieces = [
        jnp.where(row_side == 0, own, o_in),
        jnp.where(row_side == 0, o_in, own),
        second + s_in,
        third + t_in,
        fifth,
    ]
    grad_weight = jnp.concatenate([p.reshape(depth, piece) for p in pieces], axis=1)
    return (work_out, grad_projected, grad_weight)


def solution(mesh):
    placed = (
        P(("fsdp", "dp"), None),
        P(("fsdp", "dp"), None),
        P("fsdp", None),
        P(("fsdp", "dp")),
        P(("fsdp", "dp")),
    )
    sizes = (mesh.shape["fsdp"], mesh.shape["dp"])

    def local(*args):
        return body(sizes, *args)

    return jax.shard_map(
        local,
        mesh=mesh,
        in_specs=placed,
        out_specs=(P(("fsdp", "dp"), None), P(("fsdp", "dp"), None), P("fsdp", None)),
        check_vma=False,
    )
```

```python
import jax
import jax.numpy as jnp
import numpy as np
from jax import lax
from jax.experimental import pallas as pl
from jax.experimental.pallas import tpu as pltpu
from jax.sharding import PartitionSpec as P

HS = 128
GRID = 16
HALF = 64
CHUNKS = 5
NEG = -1e30
VMEM_BYTES = 48 * 1024 * 1024


def pair_table():
    index = np.arange(HALF)
    first = index < 16
    second = (index >= 16) & (index < 40)
    exponent = np.where(
        first, index / 16.0, np.where(second, (index - 16) / 24.0, (index - 40) / 24.0)
    )
    which = np.where(first, 0, np.where(second, 1, 2))
    return (100.0 ** (-exponent), which)


def angles(tube_index):
    frequency, which = pair_table()
    temporal = (tube_index // (GRID * GRID)).astype(jnp.float32)[:, None]
    vertical = (tube_index // GRID % GRID).astype(jnp.float32)[:, None]
    lateral = (tube_index % GRID).astype(jnp.float32)[:, None]
    which = jnp.asarray(which)[None, :]
    coords = jnp.where(which == 0, temporal, jnp.where(which == 1, vertical, lateral))
    angle = coords * jnp.asarray(frequency, dtype=jnp.float32)[None, :]
    cosine, sine = jnp.cos(angle), jnp.sin(angle)
    return (
        jnp.concatenate([cosine, cosine], axis=1),
        jnp.concatenate([-sine, sine], axis=1),
    )


def rotate(values, cosine, sine):
    wide = values.astype(jnp.float32)
    return wide * cosine + pltpu.roll(wide, HALF, 1) * sine


def unrotate(grads, cosine, sine):
    return grads * cosine - pltpu.roll(grads, HALF, 1) * sine


def windows(counts_ref, rows):
    first, second = counts_ref[0], counts_ref[1]
    half = rows // 2
    wide = half + 16
    start = jnp.minimum(first // 16 * 16, rows - wide)
    return (
        (0, half, 0, first),
        (pl.multiple_of(start, 16), wide, first, first + second),
    )


def probs_t(keys, query, start, low, high, scale):
    scores = (
        lax.dot_general(
            keys, query, (((1,), (1,)), ((), ())), preferred_element_type=jnp.float32
        )
        * scale
    )
    place = start + lax.broadcasted_iota(jnp.int32, (keys.shape[0], 1), 0)
    scores = jnp.where((place >= low) & (place < high), scores, NEG)
    lifted = jnp.exp(scores - jnp.max(scores, axis=0, keepdims=True))
    return lifted * (1.0 / jnp.sum(lifted, axis=0, keepdims=True))


def forward_kernel(
    counts_ref, q_ref, k_ref, v_ref, cos_ref, sin_ref, out_ref, qr, kr, total
):
    rows = q_ref.shape[0]
    scale = HS ** (-0.5)
    cosine, sine = cos_ref[...], sin_ref[...]
    qr[...] = rotate(q_ref[...], cosine, sine).astype(jnp.bfloat16)
    kr[...] = rotate(k_ref[...], cosine, sine).astype(jnp.bfloat16)
    total[...] = jnp.zeros_like(total)
    for start, wide, low, high in windows(counts_ref, rows):
        span = pl.ds(start, wide)
        probs = probs_t(kr[span, :], qr[span, :], start, low, high, scale)
        mixed = lax.dot_general(
            v_ref[span, :],
            probs.astype(jnp.bfloat16),
            (((0,), (0,)), ((), ())),
            preferred_element_type=jnp.float32,
        ).T
        place = start + lax.broadcasted_iota(jnp.int32, (wide, 1), 0)
        total[span, :] += jnp.where((place >= low) & (place < high), mixed, 0.0)
    out_ref[...] = total[...].T.astype(jnp.bfloat16)


def backward_kernel(
    counts_ref, q_ref, k_ref, v_ref, g_ref, cos_ref, sin_ref, out_ref, qr, kr, go, total, low_out
):
    part = pl.program_id(1)

    @pl.when(part == 0)
    def _():
        rows = q_ref.shape[0]
        scale = HS ** (-0.5)
        cosine, sine = cos_ref[...], sin_ref[...]
        qr[...] = rotate(q_ref[...], cosine, sine).astype(jnp.bfloat16)
        kr[...] = rotate(k_ref[...], cosine, sine).astype(jnp.bfloat16)
        go[...] = g_ref[...].astype(jnp.float32).T.astype(jnp.bfloat16)
        total[...] = jnp.zeros_like(total)
        for start, wide, low, high in windows(counts_ref, rows):
            span = pl.ds(start, wide)
            keys, query, values = kr[span, :], qr[span, :], v_ref[span, :]
            place = start + lax.broadcasted_iota(jnp.int32, (wide, 1), 0)
            grad = jnp.where(
                (place >= low) & (place < high), go[span, :].astype(jnp.float32), 0.0
            ).astype(jnp.bfloat16)
            probs = probs_t(keys, query, start, low, high, scale)
            total[2, span, :] += jnp.dot(
                probs.astype(jnp.bfloat16), grad, preferred_element_type=jnp.float32
            )
            grad_probs = lax.dot_general(
                values, grad, (((1,), (1,)), ((), ())), preferred_element_type=jnp.float32
            )
            centre = jnp.sum(probs * grad_probs, axis=0, keepdims=True)
            grad_scores = (probs * (grad_probs - centre) * scale).astype(jnp.bfloat16)
            total[1, span, :] += jnp.dot(grad_scores, query, preferred_element_type=jnp.float32)
            total[0, span, :] += lax.dot_general(
                keys, grad_scores, (((0,), (0,)), ((), ())), preferred_element_type=jnp.float32
            ).T
        low_out[0] = unrotate(total[0], cosine, sine).astype(jnp.bfloat16)
        low_out[1] = unrotate(total[1], cosine, sine).astype(jnp.bfloat16)
        low_out[2] = total[2].astype(jnp.bfloat16)

    out_ref[...] = low_out[part]


def attention_forward(projected, clip_counts, cosine, sine):
    rows = projected.shape[0]
    heads = projected.shape[1] // 3 // HS
    whole = pl.BlockSpec((rows, HS), lambda h, c: (0, 0))
    return pl.pallas_call(
        forward_kernel,
        grid_spec=pltpu.PrefetchScalarGridSpec(
            num_scalar_prefetch=1,
            grid=(heads,),
            in_specs=[
                pl.BlockSpec((rows, HS), lambda h, c: (0, h)),
                pl.BlockSpec((rows, HS), lambda h, c: (0, h + heads)),
                pl.BlockSpec((rows, HS), lambda h, c: (0, h + 2 * heads)),
                whole,
                whole,
            ],
            out_specs=pl.BlockSpec((HS, rows), lambda h, c: (h, 0)),
            scratch_shapes=[
                pltpu.VMEM((rows, HS), jnp.bfloat16),
                pltpu.VMEM((rows, HS), jnp.bfloat16),
                pltpu.VMEM((rows, HS), jnp.float32),
            ],
        ),
        out_shape=jax.ShapeDtypeStruct((heads * HS, rows), jnp.bfloat16),
        compiler_params=pltpu.CompilerParams(vmem_limit_bytes=VMEM_BYTES),
        cost_estimate=pl.CostEstimate(
            flops=heads * rows * rows * HS * 6, bytes_accessed=rows * heads * HS * 8,
            transcendentals=heads * rows * rows,
        ),
    )(clip_counts, projected, projected, projected, cosine, sine)


def attention_backward(projected, clip_counts, grad_t, cosine, sine, heads_from, heads_to, before):
    rows = projected.shape[0]
    heads = projected.shape[1] // 3 // HS
    count = heads_to - heads_from
    whole = pl.BlockSpec((rows, HS), lambda h, j, c: (0, 0))
    at = heads_from
    in_specs = [
        pl.BlockSpec((rows, HS), lambda h, j, c: (0, at + h)),
        pl.BlockSpec((rows, HS), lambda h, j, c: (0, at + h + heads)),
        pl.BlockSpec((rows, HS), lambda h, j, c: (0, at + h + 2 * heads)),
        pl.BlockSpec((HS, rows), lambda h, j, c: (at + h, 0)),
        whole,
        whole,
    ]
    operands = [clip_counts, projected, projected, projected, grad_t, cosine, sine]
    kernel, aliases = backward_kernel, {}
    if before is not None:
        in_specs.append(pl.BlockSpec(memory_space=pl.ANY))
        aliases = {len(operands): 0}
        operands.append(before)

        def kernel(*refs):
            backward_kernel(*refs[:7], *refs[8:])

    return pl.pallas_call(
        kernel,
        grid_spec=pltpu.PrefetchScalarGridSpec(
            num_scalar_prefetch=1,
            grid=(count, 3),
            in_specs=in_specs,
            out_specs=pl.BlockSpec((rows, HS), lambda h, j, c: (0, j * heads + at + h)),
            scratch_shapes=[
                pltpu.VMEM((rows, HS), jnp.bfloat16),
                pltpu.VMEM((rows, HS), jnp.bfloat16),
                pltpu.VMEM((rows, HS), jnp.bfloat16),
                pltpu.VMEM((3, rows, HS), jnp.float32),
                pltpu.VMEM((3, rows, HS), jnp.bfloat16),
            ],
        ),
        out_shape=jax.ShapeDtypeStruct(projected.shape, jnp.bfloat16),
        input_output_aliases=aliases,
        compiler_params=pltpu.CompilerParams(vmem_limit_bytes=VMEM_BYTES),
        cost_estimate=pl.CostEstimate(
            flops=count * rows * rows * HS * 70, bytes_accessed=rows * count * HS * 14,
            transcendentals=count * rows * rows,
        ),
    )(*operands)


def body(sizes, projected, cotangent, out_weight, clip_counts, tube_index):
    devices, pair = sizes
    bits = devices.bit_length() - 1
    rows = projected.shape[0]
    head_width = projected.shape[1] // 3
    heads = head_width // HS
    depth = out_weight.shape[0]
    width = out_weight.shape[1]
    piece = width // CHUNKS
    me = lax.axis_index("fsdp")
    row_side = lax.axis_index("dp")

    def across(array, bit):
        if bit < 0:
            return lax.ppermute(array, "dp", [(i, i ^ 1) for i in range(pair)])
        return lax.ppermute(array, "fsdp", [(i, i ^ (1 << bit)) for i in range(devices)])

    slot_of = [int(format(i, f"0{bits}b")[::-1], 2) for i in range(devices)]

    def to_places(array):
        return jnp.concatenate(
            [lax.dynamic_slice_in_dim(array, (p ^ me) * depth, depth, 0) for p in slot_of],
            axis=0,
        )

    def part_of(array, bit, which):
        return lax.slice_in_dim(array, which, which + 1, axis=bit)

    def together(sends, work_in, work):
        arrays, work_in = lax.optimization_barrier(([a for a, _ in sends], work_in))
        arrived = [across(a, bit) for a, (_, bit) in zip(arrays, sends)]
        return lax.optimization_barrier((arrived, work(work_in)))

    full_weight = lax.all_gather(out_weight.astype(jnp.bfloat16), "fsdp", axis=0, tiled=True)
    bounds = jnp.cumsum(clip_counts)
    live_rows = (jnp.arange(rows) < bounds[-1]).astype(jnp.bfloat16)[:, None]
    cosine, sine = angles(tube_index)
    masked_cot = cotangent * live_rows
    attn_t = attention_forward(projected, clip_counts, cosine, sine)
    placed_t = to_places(attn_t)
    half = head_width // 2
    keep_t, send_t = placed_t[:half], placed_t[half:]
    cubes = (1,) + (2,) * (bits - 1) + (depth, piece)

    def product(left, index):
        cot = lax.dynamic_slice_in_dim(masked_cot, index * piece, piece, 1)
        return jnp.dot(left, cot, preferred_element_type=jnp.float32)

    def first_sum(index):
        sent = across(product(send_t, index), 0)
        return (product(keep_t, index) + sent).reshape(cubes)

    x, near, far = 1, 2, list(range(3, bits))
    last = far[-1] if far else None
    give = first_sum(1 - row_side)
    second = first_sum(2)
    fifth = first_sum(4)
    own = first_sum(row_side)
    third = first_sum(3)

    def nothing(value):
        return value

    def step(array, bit):
        return part_of(array, bit, 0), part_of(array, bit, 1)

    def middle(array):
        for bit in far[:-1]:
            low, high = step(array, bit)
            array = low + across(high, bit)
        return array

    (g_in, s_in, t_in, f_in), _ = together(
        [
            (give, -1),
            (part_of(second, x, 1), x),
            (part_of(third, x, 1), x),
            (part_of(fifth, near, 1), near),
        ],
        (),
        nothing,
    )
    own = own + g_in
    second = part_of(second, x, 0) + s_in
    third = part_of(third, x, 0) + t_in
    fifth = middle(part_of(fifth, near, 0) + f_in)

    def grad_of(weight):
        return lax.dot_general(
            weight, masked_cot, (((1,), (1,)), ((), ())), preferred_element_type=jnp.float32
        ).astype(jnp.bfloat16)

    cuts = (0, heads * 5 // 13, heads * 11 // 13, heads)

    def backward(grad_t, index, before):
        return attention_backward(
            projected, clip_counts, grad_t, cosine, sine, cuts[index], cuts[index + 1], before
        )

    def work_one(weight):
        grad_t = grad_of(weight)
        return grad_t, backward(grad_t, 0, None)

    (o_in, s_in, f_in), (grad_t, grad_projected) = together(
        [
            (part_of(own, near, 1), near),
            (part_of(second, near, 1), near),
            (part_of(fifth, last, 1), last),
        ],
        full_weight,
        work_one,
    )
    own = middle(part_of(own, near, 0) + o_in)
    second = middle(part_of(second, near, 0) + s_in)
    fifth = part_of(fifth, last, 0) + f_in
    (o_in, s_in, t_in, f_in), (grad_t, grad_projected) = together(
        [
            (part_of(own, last, 1), last),
            (part_of(second, last, 1), last),
            (part_of(third, near, 1), near),
            (part_of(fifth, x, 1), x),
        ],
        (grad_t, grad_projected),
        lambda held: (held[0], backward(held[0], 1, held[1])),
    )
    own = part_of(own, last, 0) + o_in
    second = part_of(second, last, 0) + s_in
    third = middle(part_of(third, near, 0) + t_in)
    fifth = part_of(fifth, x, 0) + f_in
    (o_in, s_in, t_in, f_in), grad_projected = together(
        [
            (part_of(own, x, 1), x),
            (second, -1),
            (part_of(third, last, 1), last),
            (fifth, -1),
        ],
        (grad_t, grad_projected),
        lambda held: backward(held[0], 2, held[1]),
    )
    own = part_of(own, x, 0) + o_in
    second = second + s_in
    third = part_of(third, last, 0) + t_in
    fifth = fifth + f_in
    (o_in, t_in), work_out = together(
        [(own, -1), (third, -1)],
        (attn_t, full_weight),
        lambda held: lax.dot_general(
            held[0], held[1], (((0,), (0,)), ((), ())), preferred_element_type=jnp.float32
        ).astype(jnp.bfloat16),
    )
    pieces = [
        jnp.where(row_side == 0, own, o_in),
        jnp.where(row_side == 0, o_in, own),
        second,
        third + t_in,
        fifth,
    ]
    grad_weight = jnp.concatenate([p.reshape(depth, piece) for p in pieces], axis=1)
    return (work_out, grad_projected, grad_weight)


def solution(mesh):
    placed = (
        P(("fsdp", "dp"), None),
        P(("fsdp", "dp"), None),
        P("fsdp", None),
        P(("fsdp", "dp")),
        P(("fsdp", "dp")),
    )
    sizes = (mesh.shape["fsdp"], mesh.shape["dp"])

    def local(*args):
        return body(sizes, *args)

    return jax.shard_map(
        local,
        mesh=mesh,
        in_specs=placed,
        out_specs=(P(("fsdp", "dp"), None), P(("fsdp", "dp"), None), P("fsdp", None)),
        check_vma=False,
    )
```

```python
import jax
import jax.numpy as jnp
import numpy as np
from jax import lax
from jax.experimental import pallas as pl
from jax.experimental.pallas import tpu as pltpu
from jax.sharding import PartitionSpec as P

HS = 128
GRID = 16
HALF = 64
CHUNKS = 5
NEG = -1e30
VMEM_BYTES = 48 * 1024 * 1024


def pair_table():
    index = np.arange(HALF)
    first = index < 16
    second = (index >= 16) & (index < 40)
    exponent = np.where(
        first, index / 16.0, np.where(second, (index - 16) / 24.0, (index - 40) / 24.0)
    )
    which = np.where(first, 0, np.where(second, 1, 2))
    return (100.0 ** (-exponent), which)


def angles(tube_index):
    frequency, which = pair_table()
    temporal = (tube_index // (GRID * GRID)).astype(jnp.float32)[:, None]
    vertical = (tube_index // GRID % GRID).astype(jnp.float32)[:, None]
    lateral = (tube_index % GRID).astype(jnp.float32)[:, None]
    which = jnp.asarray(which)[None, :]
    coords = jnp.where(which == 0, temporal, jnp.where(which == 1, vertical, lateral))
    angle = coords * jnp.asarray(frequency, dtype=jnp.float32)[None, :]
    cosine, sine = jnp.cos(angle), jnp.sin(angle)
    return (
        jnp.concatenate([cosine, cosine], axis=1),
        jnp.concatenate([-sine, sine], axis=1),
    )


def rotate(values, cosine, sine):
    wide = values.astype(jnp.float32)
    return wide * cosine + pltpu.roll(wide, HALF, 1) * sine


def unrotate(grads, cosine, sine):
    return grads * cosine - pltpu.roll(grads, HALF, 1) * sine


def windows(counts_ref, rows):
    first, second = counts_ref[0], counts_ref[1]
    half = rows // 2
    wide = half + 16
    start = jnp.minimum(first // 16 * 16, rows - wide)
    return (
        (0, half, 0, first),
        (pl.multiple_of(start, 16), wide, first, first + second),
    )


def probs_t(keys, query, start, low, high, scale):
    scores = (
        lax.dot_general(
            keys, query, (((1,), (1,)), ((), ())), preferred_element_type=jnp.float32
        )
        * scale
    )
    place = start + lax.broadcasted_iota(jnp.int32, (keys.shape[0], 1), 0)
    scores = jnp.where((place >= low) & (place < high), scores, NEG)
    lifted = jnp.exp(scores - jnp.max(scores, axis=0, keepdims=True))
    return lifted * (1.0 / jnp.sum(lifted, axis=0, keepdims=True))


def forward_kernel(
    counts_ref, q_ref, k_ref, v_ref, cos_ref, sin_ref, out_ref, qr, kr, total
):
    rows = q_ref.shape[0]
    scale = HS ** (-0.5)
    cosine, sine = cos_ref[...], sin_ref[...]
    qr[...] = rotate(q_ref[...], cosine, sine).astype(jnp.bfloat16)
    kr[...] = rotate(k_ref[...], cosine, sine).astype(jnp.bfloat16)
    total[...] = jnp.zeros_like(total)
    for start, wide, low, high in windows(counts_ref, rows):
        span = pl.ds(start, wide)
        probs = probs_t(kr[span, :], qr[span, :], start, low, high, scale)
        mixed = lax.dot_general(
            v_ref[span, :],
            probs.astype(jnp.bfloat16),
            (((0,), (0,)), ((), ())),
            preferred_element_type=jnp.float32,
        ).T
        place = start + lax.broadcasted_iota(jnp.int32, (wide, 1), 0)
        total[span, :] += jnp.where((place >= low) & (place < high), mixed, 0.0)
    out_ref[...] = total[...].T.astype(jnp.bfloat16)


def backward_kernel(
    counts_ref, q_ref, k_ref, v_ref, g_ref, cos_ref, sin_ref, out_ref, qr, kr, go, total, low_out
):
    part = pl.program_id(1)

    @pl.when(part == 0)
    def _():
        rows = q_ref.shape[0]
        scale = HS ** (-0.5)
        cosine, sine = cos_ref[...], sin_ref[...]
        qr[...] = rotate(q_ref[...], cosine, sine).astype(jnp.bfloat16)
        kr[...] = rotate(k_ref[...], cosine, sine).astype(jnp.bfloat16)
        go[...] = g_ref[...].astype(jnp.float32).T.astype(jnp.bfloat16)
        total[...] = jnp.zeros_like(total)
        for start, wide, low, high in windows(counts_ref, rows):
            span = pl.ds(start, wide)
            keys, query, values = kr[span, :], qr[span, :], v_ref[span, :]
            place = start + lax.broadcasted_iota(jnp.int32, (wide, 1), 0)
            grad = jnp.where(
                (place >= low) & (place < high), go[span, :].astype(jnp.float32), 0.0
            ).astype(jnp.bfloat16)
            probs = probs_t(keys, query, start, low, high, scale)
            total[2, span, :] += jnp.dot(
                probs.astype(jnp.bfloat16), grad, preferred_element_type=jnp.float32
            )
            grad_probs = lax.dot_general(
                values, grad, (((1,), (1,)), ((), ())), preferred_element_type=jnp.float32
            )
            centre = jnp.sum(probs * grad_probs, axis=0, keepdims=True)
            grad_scores = (probs * (grad_probs - centre) * scale).astype(jnp.bfloat16)
            total[1, span, :] += jnp.dot(grad_scores, query, preferred_element_type=jnp.float32)
            total[0, span, :] += lax.dot_general(
                keys, grad_scores, (((0,), (0,)), ((), ())), preferred_element_type=jnp.float32
            ).T
        low_out[0] = unrotate(total[0], cosine, sine).astype(jnp.bfloat16)
        low_out[1] = unrotate(total[1], cosine, sine).astype(jnp.bfloat16)
        low_out[2] = total[2].astype(jnp.bfloat16)

    out_ref[...] = low_out[part]


def attention_forward(projected, clip_counts, cosine, sine):
    rows = projected.shape[0]
    heads = projected.shape[1] // 3 // HS
    whole = pl.BlockSpec((rows, HS), lambda h, c: (0, 0))
    return pl.pallas_call(
        forward_kernel,
        grid_spec=pltpu.PrefetchScalarGridSpec(
            num_scalar_prefetch=1,
            grid=(heads,),
            in_specs=[
                pl.BlockSpec((rows, HS), lambda h, c: (0, h)),
                pl.BlockSpec((rows, HS), lambda h, c: (0, h + heads)),
                pl.BlockSpec((rows, HS), lambda h, c: (0, h + 2 * heads)),
                whole,
                whole,
            ],
            out_specs=pl.BlockSpec((HS, rows), lambda h, c: (h, 0)),
            scratch_shapes=[
                pltpu.VMEM((rows, HS), jnp.bfloat16),
                pltpu.VMEM((rows, HS), jnp.bfloat16),
                pltpu.VMEM((rows, HS), jnp.float32),
            ],
        ),
        out_shape=jax.ShapeDtypeStruct((heads * HS, rows), jnp.bfloat16),
        compiler_params=pltpu.CompilerParams(vmem_limit_bytes=VMEM_BYTES),
        cost_estimate=pl.CostEstimate(
            flops=heads * rows * rows * HS * 6, bytes_accessed=rows * heads * HS * 8,
            transcendentals=heads * rows * rows,
        ),
    )(clip_counts, projected, projected, projected, cosine, sine)


def attention_backward(projected, clip_counts, grad_t, cosine, sine, heads_from, heads_to, before):
    rows = projected.shape[0]
    heads = projected.shape[1] // 3 // HS
    count = heads_to - heads_from
    whole = pl.BlockSpec((rows, HS), lambda h, j, c: (0, 0))
    at = heads_from
    in_specs = [
        pl.BlockSpec((rows, HS), lambda h, j, c: (0, at + h)),
        pl.BlockSpec((rows, HS), lambda h, j, c: (0, at + h + heads)),
        pl.BlockSpec((rows, HS), lambda h, j, c: (0, at + h + 2 * heads)),
        pl.BlockSpec((HS, rows), lambda h, j, c: (at + h, 0)),
        whole,
        whole,
    ]
    operands = [clip_counts, projected, projected, projected, grad_t, cosine, sine]
    kernel, aliases = backward_kernel, {}
    if before is not None:
        in_specs.append(pl.BlockSpec(memory_space=pl.ANY))
        aliases = {len(operands): 0}
        operands.append(before)

        def kernel(*refs):
            backward_kernel(*refs[:7], *refs[8:])

    return pl.pallas_call(
        kernel,
        grid_spec=pltpu.PrefetchScalarGridSpec(
            num_scalar_prefetch=1,
            grid=(count, 3),
            in_specs=in_specs,
            out_specs=pl.BlockSpec((rows, HS), lambda h, j, c: (0, j * heads + at + h)),
            scratch_shapes=[
                pltpu.VMEM((rows, HS), jnp.bfloat16),
                pltpu.VMEM((rows, HS), jnp.bfloat16),
                pltpu.VMEM((rows, HS), jnp.bfloat16),
                pltpu.VMEM((3, rows, HS), jnp.float32),
                pltpu.VMEM((3, rows, HS), jnp.bfloat16),
            ],
        ),
        out_shape=jax.ShapeDtypeStruct(projected.shape, jnp.bfloat16),
        input_output_aliases=aliases,
        compiler_params=pltpu.CompilerParams(vmem_limit_bytes=VMEM_BYTES),
        cost_estimate=pl.CostEstimate(
            flops=count * rows * rows * HS * 70, bytes_accessed=rows * count * HS * 14,
            transcendentals=count * rows * rows,
        ),
    )(*operands)


def body(sizes, projected, cotangent, out_weight, clip_counts, tube_index):
    devices, pair = sizes
    bits = devices.bit_length() - 1
    rows = projected.shape[0]
    head_width = projected.shape[1] // 3
    heads = head_width // HS
    depth = out_weight.shape[0]
    width = out_weight.shape[1]
    piece = width // CHUNKS
    me = lax.axis_index("fsdp")
    row_side = lax.axis_index("dp")

    def across(array, bit):
        if bit < 0:
            return lax.ppermute(array, "dp", [(i, i ^ 1) for i in range(pair)])
        return lax.ppermute(array, "fsdp", [(i, i ^ (1 << bit)) for i in range(devices)])

    slot_of = [int(format(i, f"0{bits}b")[::-1], 2) for i in range(devices)]

    def to_places(array):
        return jnp.concatenate(
            [lax.dynamic_slice_in_dim(array, (p ^ me) * depth, depth, 0) for p in slot_of],
            axis=0,
        )

    def part_of(array, bit, which):
        return lax.slice_in_dim(array, which, which + 1, axis=bit)

    def together(sends, work_in, work):
        arrays, work_in = lax.optimization_barrier(([a for a, _ in sends], work_in))
        arrived = [across(a, bit) for a, (_, bit) in zip(arrays, sends)]
        return lax.optimization_barrier((arrived, work(work_in)))

    full_weight = lax.all_gather(out_weight.astype(jnp.bfloat16), "fsdp", axis=0, tiled=True)
    bounds = jnp.cumsum(clip_counts)
    live_rows = (jnp.arange(rows) < bounds[-1]).astype(jnp.bfloat16)[:, None]
    cosine, sine = angles(tube_index)
    masked_cot = cotangent * live_rows
    attn_t = attention_forward(projected, clip_counts, cosine, sine)
    placed_t = to_places(attn_t)
    half = head_width // 2
    keep_t, send_t = placed_t[:half], placed_t[half:]
    cubes = (1,) + (2,) * (bits - 1) + (depth, piece)

    def product(left, index):
        cot = lax.dynamic_slice_in_dim(masked_cot, index * piece, piece, 1)
        return jnp.dot(left, cot, preferred_element_type=jnp.float32)

    def first_sum(index):
        sent = across(product(send_t, index), 0)
        return (product(keep_t, index) + sent).reshape(cubes)

    x, near, far = 1, 2, list(range(3, bits))
    last = far[-1] if far else None
    give = first_sum(1 - row_side)
    second = first_sum(2)
    fifth = first_sum(4)
    own = first_sum(row_side)
    third = first_sum(3)

    def nothing(value):
        return value

    def step(array, bit):
        return part_of(array, bit, 0), part_of(array, bit, 1)

    def middle(array):
        for bit in far[:-1]:
            low, high = step(array, bit)
            array = low + across(high, bit)
        return array

    (g_in, s_in, t_in, f_in), _ = together(
        [
            (give, -1),
            (part_of(second, x, 1), x),
            (part_of(third, x, 1), x),
            (part_of(fifth, near, 1), near),
        ],
        (),
        nothing,
    )
    own = own + g_in
    second = part_of(second, x, 0) + s_in
    third = part_of(third, x, 0) + t_in
    fifth = middle(part_of(fifth, near, 0) + f_in)

    def grad_of(weight):
        return lax.dot_general(
            weight, masked_cot, (((1,), (1,)), ((), ())), preferred_element_type=jnp.float32
        ).astype(jnp.bfloat16)

    cuts = (0, heads * 7 // 13, heads)

    def backward(grad_t, index, before):
        return attention_backward(
            projected, clip_counts, grad_t, cosine, sine, cuts[index], cuts[index + 1], before
        )

    def work_one(weight):
        grad_t = grad_of(weight)
        return grad_t, backward(grad_t, 0, None)

    (o_in, s_in, f_in), (grad_t, grad_projected) = together(
        [
            (part_of(own, near, 1), near),
            (part_of(second, near, 1), near),
            (part_of(fifth, last, 1), last),
        ],
        full_weight,
        work_one,
    )
    own = middle(part_of(own, near, 0) + o_in)
    second = middle(part_of(second, near, 0) + s_in)
    fifth = part_of(fifth, last, 0) + f_in
    (o_in, s_in, t_in, f_in), (grad_t, grad_projected) = together(
        [
            (part_of(own, last, 1), last),
            (part_of(second, last, 1), last),
            (part_of(third, near, 1), near),
            (part_of(fifth, x, 1), x),
        ],
        (grad_t, grad_projected),
        lambda held: (held[0], backward(held[0], 1, held[1])),
    )
    own = part_of(own, last, 0) + o_in
    second = part_of(second, last, 0) + s_in
    third = middle(part_of(third, near, 0) + t_in)
    fifth = part_of(fifth, x, 0) + f_in
    (o_in, s_in, t_in, f_in), work_out = together(
        [
            (part_of(own, x, 1), x),
            (second, -1),
            (part_of(third, last, 1), last),
            (fifth, -1),
        ],
        (attn_t, full_weight),
        lambda held: lax.dot_general(
            held[0], held[1], (((0,), (0,)), ((), ())), preferred_element_type=jnp.float32
        ).astype(jnp.bfloat16),
    )
    own = part_of(own, x, 0) + o_in
    second = second + s_in
    third = part_of(third, last, 0) + t_in
    fifth = fifth + f_in
    (o_in, t_in), _ = together(
        [(own, -1), (third, -1)],
        (),
        nothing,
    )
    pieces = [
        jnp.where(row_side == 0, own, o_in),
        jnp.where(row_side == 0, o_in, own),
        second,
        third + t_in,
        fifth,
    ]
    grad_weight = jnp.concatenate([p.reshape(depth, piece) for p in pieces], axis=1)
    return (work_out, grad_projected, grad_weight)


def solution(mesh):
    placed = (
        P(("fsdp", "dp"), None),
        P(("fsdp", "dp"), None),
        P("fsdp", None),
        P(("fsdp", "dp")),
        P(("fsdp", "dp")),
    )
    sizes = (mesh.shape["fsdp"], mesh.shape["dp"])

    def local(*args):
        return body(sizes, *args)

    return jax.shard_map(
        local,
        mesh=mesh,
        in_specs=placed,
        out_specs=(P(("fsdp", "dp"), None), P(("fsdp", "dp"), None), P("fsdp", None)),
        check_vma=False,
    )
```
